32 devices in a mesh: fsdp: 4 (over z), expert: 8 (over y, x, core).
Axes of the slice: x: 2, y: 2, z: 4, core: 2. Of those that a mesh axis runs over, the one named last changes fastest.
Arguments:
- tokens: bfloat16 [6304, 768], P(('fsdp', 'expert')), may hold values from -6 to 6
- cotangent: bfloat16 [6304, 768], P(('fsdp', 'expert')), may hold values from -6 to 6
- routes: int32 [6304, 2], P(('fsdp', 'expert')), may hold values from 0 to 7, all different within a row; in each aligned block of 197 rows (0 to 196, 197 to 393, ...) at most 66 rows name the same one
- ln1_gain: bfloat16 [768], P(('fsdp', 'expert')), may hold values from 0.099609375 to 1.8984375
- ln1_bias: bfloat16 [768], P(('fsdp', 'expert')), may hold values from -3 to 3
- qkv_weight: bfloat16 [768, 2304], P(('fsdp', 'expert')), may hold values from -0.21875 to 0.21875
- query_bias: bfloat16 [768], P(('fsdp', 'expert')), may hold values from -3 to 3
- value_bias: bfloat16 [768], P(('fsdp', 'expert')), may hold values from -3 to 3
- out_weight: bfloat16 [768, 768], P(('fsdp', 'expert')), may hold values from -1.75 to 1.75
- out_bias: bfloat16 [768], P(('fsdp', 'expert')), may hold values from -3 to 3
- ln2_gain: bfloat16 [768], P(('fsdp', 'expert')), may hold values from 0.099609375 to 1.8984375
- ln2_bias: bfloat16 [768], P(('fsdp', 'expert')), may hold values from -3 to 3
- router_weight: bfloat16 [768, 8], P(('fsdp', 'expert')), may hold values from -0.15625 to 0.15625
- gate_up: bfloat16 [8, 768, 2, 3072], P('expert', 'fsdp'), may hold values from -0.21875 to 0.21875
- down_weight: bfloat16 [8, 768, 3072], P('expert', 'fsdp'), may hold values from -0.625 to 0.625
Outputs:
- mixed: bfloat16 [6304, 768], P(('fsdp', 'expert'))
- token_grad: float32 [6304, 768], P(('fsdp', 'expert'))
- ln1_gain_grad: float32 [768], P(('fsdp', 'expert'))
- ln1_bias_grad: float32 [768], P(('fsdp', 'expert'))
- qkv_weight_grad: float32 [768, 2304], P(('fsdp', 'expert'))
- query_bias_grad: float32 [768], P(('fsdp', 'expert'))
- value_bias_grad: float32 [768], P(('fsdp', 'expert'))
- out_weight_grad: float32 [768, 768], P(('fsdp', 'expert'))
- out_bias_grad: float32 [768], P(('fsdp', 'expert'))
- ln2_gain_grad: float32 [768], P(('fsdp', 'expert'))
- ln2_bias_grad: float32 [768], P(('fsdp', 'expert'))
- router_weight_grad: float32 [768, 8], P(('fsdp', 'expert'))
- gate_up_grad: float32 [8, 768, 2, 3072], P('expert', 'fsdp')
- down_weight_grad: float32 [8, 768, 3072], P('expert', 'fsdp')
The draws below stay inside these ranges and needn't reach their ends.
Inputs may be any that keep to these rules, and one draw needn't show every extreme that they name: `routes`: A token's two experts differ. Among the tokens of one device no expert is named more than 66 times, and in every draw some expert is named exactly 66 times by one device's tokens.
All inputs are finite; a program needn't handle non-finite values.
Results may differ from the reference program's by a relative error of at most 0.015.
Values may be sent and summed in bfloat16 or wider, within the bound.
A program may use at most 192 MiB of HBM per device.

```python
import math
import jax
import jax.numpy as jnp
import numpy as np
from jax import lax

D = 768
HEADS = 12
HEAD_DIM = 64
FF = 3072
SEQ = 197
TOK_DEV = 197
IMAGES = 32
TOKENS = 6304
EXPERTS = 8
CAP = 66
N_FSDP = 4
N_EXPERT = 8


def with_spikes(result, rng, source, target, blocks, factor):
    def block_of(position):
        return (jnp.arange(result.shape[position]) // (result.shape[position] // blocks)).reshape((-1,) + (1,) * (result.ndim - 1 - position))

    first = jax.random.permutation(rng, blocks)[block_of(target)]
    far = (block_of(target) + blocks // 2) % blocks
    return jnp.where((block_of(source) == first) | (block_of(source) == far), factor * result, result)


def block_levels(own_key, dims, pieces, least, high):
    loudness, own = 1.0, jax.random.fold_in(own_key, 6)
    for position, shards_of in pieces:
        draws = jnp.exp(jax.random.uniform(jax.random.fold_in(own, position), (shards_of,), jnp.float32, least / len(pieces), high / len(pieces)))
        loudness = loudness * jnp.repeat(draws, dims[position] // shards_of).reshape([-1 if axis == position else 1 for axis in range(len(dims))])
    return loudness


def assign_block(stream_key, own, number, rows, number_of, top, most, lean):
    order = jax.random.permutation(stream_key, number_of)
    crowded, common = load_shares(number_of, rows * top, most, lean, True), load_shares(number_of, rows * top, most, lean, False)
    places = jnp.arange(number_of)

    def named(lengths, rotation):
        used = int((lengths > 0).sum())
        fixed = max(1, used // 4)
        passed = fixed + (places - fixed + rotation * (used - fixed)) % max(1, number_of - fixed)
        return jnp.zeros((number_of,), jnp.int32).at[order[jnp.where(places < fixed, places, passed)]].set(jnp.asarray(lengths, jnp.int32))

    lengths = jnp.where(number % 4 == 0, named(crowded, number // 4), named(common, number - number // 4 - 1))
    mixed = jax.random.permutation(jax.random.fold_in(own, 3), number_of)
    source_of, sink = mixed[0:number_of // 2 * 2:2], mixed[1:number_of // 2 * 2:2]
    slack = jnp.minimum(lengths[source_of] - 1, most - lengths[sink]) // 2
    slack = jnp.where((source_of == order[0]) | (sink == order[0]) | (lengths[sink] == 0), 0, jnp.maximum(slack, 0))
    passed = jax.random.randint(jax.random.fold_in(own, 4), (number_of // 2,), 0, 1 << 20) % (slack + 1)
    lengths = lengths.at[source_of].add(-passed).at[sink].add(passed)
    items = jnp.searchsorted(jnp.cumsum(lengths), jnp.arange(rows * top), side="right").astype(jnp.int32)
    table = items.reshape(top, rows).T
    table = table[jax.random.permutation(jax.random.fold_in(own, 1), rows)]
    rotation = jax.random.randint(jax.random.fold_in(own, 2), (rows, 1), 0, top)
    return jnp.take_along_axis(table, (jnp.arange(top)[None, :] + rotation) % top, axis=1)


def load_shares(number_of, total, most, slope, full):
    weights = [(1 << 20) // math.isqrt(grade ** slope) + 1 for grade in range(1, number_of + 1)]
    largest = most if full else min(most, max(-(-total // number_of), total * weights[0] // sum(weights)))
    least = 1 if total - largest >= number_of - 1 else 0
    holding, spare = [largest] + [least] * (number_of - 1), total - largest - least * (number_of - 1)
    while spare > 0:
        free = [i for i in range(1, number_of) if holding[i] < largest] or [i for i in range(1, number_of) if holding[i] < most]
        mass, budget = sum([weights[i] for i in free]), spare
        for i in free:
            more = min(most - holding[i], max(1, budget * weights[i] // mass), spare)
            holding[i] = holding[i] + more
            spare = spare - more
    return np.array(holding)


def bell_draw(rng, shape, spread, most, pieces=(), held_as=jnp.bfloat16):
    loudness = block_levels(rng, shape, pieces, -0.22, 0.18) if pieces else 1.0
    array = jax.random.normal(rng, shape, jnp.float32) * spread * loudness
    return jnp.minimum(jnp.maximum(array, -most), most).astype(held_as)


def heavy_noise(stream_key, dims, spread, limit, cuts, heavy, kind=jnp.bfloat16):
    array = spread * jax.random.normal(stream_key, dims, jnp.float32)
    if cuts:
        array = array * block_levels(stream_key, dims, cuts, -0.22, 0.18)
    return jnp.clip(with_spikes(array, jax.random.fold_in(stream_key, 3), *heavy), -limit, limit).astype(kind)


def setup_inputs(seed: int = 0) -> dict:
    arg_keys = jax.random.split(jax.random.key(seed), 16)
    tokens = heavy_noise(arg_keys[0], (TOKENS, D), 1.0, 6.0, ((0, 32),), (0, 1, 32, 2.75))
    cotangent = bell_draw(arg_keys[1], (TOKENS, D), 1.0, 6.0, ((0, 32),))
    routes_keys = jax.random.split(jax.random.fold_in(arg_keys[2], 1), TOKENS // TOK_DEV)
    routes_turns = jax.random.permutation(jax.random.fold_in(arg_keys[2], 3), TOKENS // TOK_DEV)
    routes = jax.vmap(lambda own, number: assign_block(jax.random.fold_in(arg_keys[2], 2), own, number, TOK_DEV, EXPERTS, 2, CAP, 2))(routes_keys, routes_turns).reshape((TOKENS, 2))
    ln1_gain = jnp.clip(1.0 + 0.18 * jax.random.normal(arg_keys[3], (D,), jnp.float32), 0.099609375, 1.8984375).astype(jnp.bfloat16)
    ln1_bias = bell_draw(arg_keys[4], (D,), 0.5, 3.0, ((0, 32),))
    qkv_weight = bell_draw(arg_keys[5], (D, 3 * D), D ** -0.5, 0.21875, ((0, 32),))
    query_bias = bell_draw(arg_keys[6], (D,), 0.5, 3.0, ((0, 32),))
    value_bias = bell_draw(arg_keys[7], (D,), 0.5, 3.0, ((0, 32),))
    out_weight = bell_draw(arg_keys[8], (D, D), (D // 64) ** -0.5, 1.75, ((0, 32),))
    out_bias = bell_draw(arg_keys[9], (D,), 0.5, 3.0, ((0, 32),))
    ln2_gain = jnp.clip(1.0 + 0.18 * jax.random.normal(arg_keys[10], (D,), jnp.float32), 0.099609375, 1.8984375).astype(jnp.bfloat16)
    ln2_bias = bell_draw(arg_keys[11], (D,), 0.5, 3.0, ((0, 32),))
    router_weight = bell_draw(arg_keys[12], (D, EXPERTS), (2 * D) ** -0.5, 0.15625, ((0, 32),))
    gate_up = bell_draw(arg_keys[13], (EXPERTS, D, 2, FF), D ** -0.5, 0.21875, ((0, 8), (1, 4)))
    down_weight = bell_draw(arg_keys[14], (EXPERTS, D, FF), (max(2 * FF // (EXPERTS * EXPERTS), 1)) ** -0.5, 0.625, ((0, 8), (1, 4)))
    return {"tokens": tokens, "cotangent": cotangent, "routes": routes, "ln1_gain": ln1_gain, "ln1_bias": ln1_bias, "qkv_weight": qkv_weight, "query_bias": query_bias, "value_bias": value_bias, "out_weight": out_weight, "out_bias": out_bias, "ln2_gain": ln2_gain, "ln2_bias": ln2_bias, "router_weight": router_weight, "gate_up": gate_up, "down_weight": down_weight}


HIGHEST = lax.Precision.HIGHEST
EPSILON = 1e-06

@jax.custom_vjp
def low(v):
    return lax.optimization_barrier(v.astype(jnp.bfloat16)).astype(jnp.float32)

@jax.custom_vjp
def low_back(v):
    return v

def low_keep(v):
    return (low(v), None)

def low_pass(kept, grad):
    return (grad,)

def back_keep(v):
    return (v, None)

def back_low(kept, grad):
    return (low(grad),)
low.defvjp(low_keep, low_pass)
low_back.defvjp(back_keep, back_low)

def layer_norm(values, gain_vec, shift_vec):
    row_mean = lax.optimization_barrier(jnp.mean(values, -1, keepdims=True))
    centered = values - row_mean
    row_var = lax.optimization_barrier(jnp.mean(centered * centered, -1, keepdims=True))
    return centered * lax.rsqrt(row_var + EPSILON) * gain_vec + shift_vec

def softmax_rows(scores):
    largest = lax.optimization_barrier(jnp.max(scores, -1, keepdims=True))
    raised = jnp.exp(scores - largest)
    return raised / lax.optimization_barrier(jnp.sum(raised, -1, keepdims=True))

def slot_positions(routes):
    per_block = routes.reshape(TOKENS // TOK_DEV, TOK_DEV * 2)
    member = (per_block[:, :, None] == jnp.arange(EXPERTS, dtype=jnp.int32)[None, None, :]).astype(jnp.int32)
    before = jnp.cumsum(member, 1) - member
    return lax.optimization_barrier(jnp.sum(before * member, 2)).reshape(TOKENS, 2).astype(jnp.int32)

def attend(packed):
    queries, keys_all, values_all = packed
    raw_scores = jnp.einsum('gqhc,gkhc->ghqk', queries, keys_all, precision=HIGHEST) * HEAD_DIM ** (-0.5)
    weights = low(softmax_rows(low_back(raw_scores)))
    return low_back(low(jnp.einsum('ghqk,gkhc->gqhc', weights, values_all, precision=HIGHEST)))

def expert_rows(packed):
    row_block, pair_mat, down_mat = packed
    pair_out = low_back(jnp.dot(row_block, pair_mat.reshape(D, 2 * FF), precision=HIGHEST))
    hidden = low(jax.nn.gelu(pair_out[:, :FF], approximate=False) * pair_out[:, FF:])
    return low_back(low(jnp.dot(hidden, down_mat.T, precision=HIGHEST)))

def forward(tokens, ln1_gain, ln1_bias, qkv_weight, query_bias, value_bias, out_weight, out_bias, ln2_gain, ln2_bias, router_weight, gate_up, down_weight, routes, slot_index):
    normalized_first = low(layer_norm(tokens, ln1_gain, ln1_bias))
    bias_row = jnp.concatenate([query_bias, jnp.zeros_like(query_bias), value_bias])
    projected = low_back(low(jnp.dot(normalized_first, qkv_weight, precision=HIGHEST) + bias_row))
    group_size = math.gcd(IMAGES, 16)
    split_heads = projected.reshape(IMAGES // group_size, group_size, SEQ, 3, HEADS, HEAD_DIM)
    attended = lax.map(jax.checkpoint(attend), (split_heads[:, :, :, 0], split_heads[:, :, :, 1], split_heads[:, :, :, 2]))
    attended = attended.reshape(TOKENS, D)
    branch = low_back(jnp.dot(attended, out_weight, precision=HIGHEST) + out_bias)
    resid_mid = tokens + branch
    normalized_second = low(layer_norm(resid_mid, ln2_gain, ln2_bias))
    logits = low_back(jnp.dot(normalized_second, router_weight, precision=HIGHEST))
    gate_probs = softmax_rows(logits)
    picked = jnp.take_along_axis(gate_probs, routes, 1)
    block_count = N_FSDP * N_EXPERT
    owner_block = jnp.broadcast_to((jnp.arange(TOKENS, dtype=jnp.int32) // TOK_DEV)[:, None], (TOKENS, 2))
    sent_rows = jnp.broadcast_to(normalized_second[:, None, :], (TOKENS, 2, D))
    buffer = jnp.zeros((block_count, EXPERTS, CAP, D), jnp.float32).at[owner_block, routes, slot_index].add(sent_rows)
    buffer = low_back(buffer)
    per_expert = jnp.transpose(buffer, (1, 0, 2, 3)).reshape(EXPERTS, block_count * CAP, D)
    expert_out = lax.map(jax.checkpoint(expert_rows), (per_expert, gate_up, down_weight))
    expert_out = jnp.transpose(expert_out.reshape(EXPERTS, block_count, CAP, D), (1, 0, 2, 3))
    chosen = expert_out[owner_block, routes, slot_index]
    return resid_mid + lax.optimization_barrier(jnp.sum(picked[:, :, None] * chosen, 1))

def reference(tokens, cotangent, routes, ln1_gain, ln1_bias, qkv_weight, query_bias, value_bias, out_weight, out_bias, ln2_gain, ln2_bias, router_weight, gate_up, down_weight):
    slot_index = slot_positions(routes)
    floats = tuple((item.astype(jnp.float32) for item in (tokens, ln1_gain, ln1_bias, qkv_weight, query_bias, value_bias, out_weight, out_bias, ln2_gain, ln2_bias, router_weight, gate_up, down_weight)))

    def forward_of(*values):
        return forward(*values, routes, slot_index)
    mixed_out, pull_back = jax.vjp(forward_of, *floats)
    gradients = pull_back(cotangent.astype(jnp.float32))
    return (mixed_out.astype(jnp.bfloat16), gradients[0], gradients[1], gradients[2], gradients[3], gradients[4], gradients[5], gradients[6], gradients[7], gradients[8], gradients[9], gradients[10], gradients[11], gradients[12])
```

```python
import jax
import jax.numpy as jnp
from jax import lax
from jax.sharding import PartitionSpec as P

HEADS = 12
HEAD_DIM = 64
SEQ = 197


EPSILON = 1e-06


def matmul_transposed(first_op, second_op):
    return lax.dot_general(
        first_op, second_op, (((1,), (1,)), ((), ())), preferred_element_type=jnp.float32
    )


def transposed_matmul(first_op, second_op):
    return lax.dot_general(
        first_op, second_op, (((0,), (0,)), ((), ())), preferred_element_type=jnp.float32
    )


def softmax_rows(scores):
    largest = jnp.max(scores, -1, keepdims=True)
    raised = jnp.exp(scores - largest)
    return raised / jnp.sum(raised, -1, keepdims=True)


def layer_norm_apply(values, gain_vec, shift_vec):
    row_mean = jnp.mean(values, -1, keepdims=True)
    centered = values - row_mean
    inv_std = lax.rsqrt(jnp.mean(centered * centered, -1, keepdims=True) + EPSILON)
    normed = centered * inv_std
    return (normed * gain_vec + shift_vec, normed, inv_std)


def norm_backward(grad_in, gain_vec, normed, inv_std):
    scaled = grad_in * gain_vec
    mean_one = jnp.mean(scaled, -1, keepdims=True)
    mean_two = jnp.mean(scaled * normed, -1, keepdims=True)
    grad_values = inv_std * (scaled - mean_one - normed * mean_two)
    return (grad_values, jnp.sum(grad_in * normed, 0), jnp.sum(grad_in, 0))


def gated_unit(pair_out):
    half_width = pair_out.shape[1] // 2
    return jax.nn.gelu(pair_out[:, :half_width], approximate=False) * pair_out[:, half_width:]


def exchange(blocks, axis_name):
    return lax.all_to_all(blocks, axis_name, split_axis=0, concat_axis=0, tiled=True)


def sum_blocks(blocks, axis_name):
    return jnp.sum(exchange(blocks, axis_name).astype(jnp.float32), 0)


def owners_sum(grad):
    outer, inner = lax.axis_size("fsdp"), lax.axis_size("expert")
    rows = grad.shape[0] // (outer * inner)
    parts = grad.astype(jnp.bfloat16).reshape(outer, inner, rows, grad.shape[1])
    half = sum_blocks(parts.transpose(1, 0, 2, 3), "expert")
    return sum_blocks(half.astype(jnp.bfloat16), "fsdp")


def owners_sum_columns(grad):
    outer, inner = lax.axis_size("fsdp"), lax.axis_size("expert")
    count = grad.shape[0]
    parts = grad.reshape(count, outer, inner, grad.shape[1] // (outer * inner))
    half = sum_blocks(parts.transpose(2, 1, 0, 3), "expert")
    return sum_blocks(half, "fsdp")


def per_device(
    tokens,
    cotangent,
    routes,
    ln1_gain,
    ln1_bias,
    qkv_weight,
    query_bias,
    value_bias,
    out_weight,
    out_bias,
    ln2_gain,
    ln2_bias,
    router_weight,
    gate_up,
    down_weight,
):
    tok_count = tokens.shape[0]
    feature_count = tokens.shape[1]
    images = tok_count // SEQ
    score_scale = HEAD_DIM ** (-0.5)
    fsdp = lax.axis_size("fsdp")
    qkv_width, out_width = qkv_weight.shape[1], out_weight.shape[1]
    experts = router_weight.shape[1]
    hidden_width = gate_up.shape[3]
    shard_width = hidden_width // fsdp
    shard_rows = gate_up.shape[1]
    vectors = jnp.stack(
        [ln1_gain, ln1_bias, query_bias, value_bias, out_bias, ln2_gain, ln2_bias], 1
    )
    small = jnp.concatenate([router_weight, vectors], 1)
    small = jnp.pad(small, ((0, 0), (0, -small.shape[1] % 128)))
    packed = lax.all_gather(
        jnp.concatenate([qkv_weight, out_weight, small], 1),
        ("fsdp", "expert"),
        axis=0,
        tiled=True,
    )
    qkv_full = packed[:, :qkv_width]
    out_full = packed[:, qkv_width : qkv_width + out_width]
    small_full = packed[:, qkv_width + out_width :]
    router_full = small_full[:, :experts]
    gain_one, shift_one, query_shift, value_shift, out_shift, gain_two, shift_two = (
        small_full[:, experts : experts + 7].T
    )
    up_parts = gate_up[0].reshape(shard_rows, 2, fsdp, shard_width).transpose(2, 0, 1, 3)
    up_full = exchange(up_parts.reshape(fsdp, shard_rows, 2 * shard_width), "fsdp")
    up_full = up_full.reshape(feature_count, 2 * shard_width)
    down_parts = down_weight[0].reshape(shard_rows, fsdp, shard_width).transpose(1, 0, 2)
    down_full = exchange(down_parts, "fsdp").reshape(feature_count, shard_width)
    resid_in = tokens.astype(jnp.float32)
    normalized_first, standardized_first, inverse_deviation_first = layer_norm_apply(
        resid_in, gain_one.astype(jnp.float32), shift_one.astype(jnp.float32)
    )
    normalized_first = normalized_first.astype(jnp.bfloat16)
    proj_shift = jnp.concatenate([query_shift, jnp.zeros_like(query_shift), value_shift]).astype(
        jnp.float32
    )
    projected = (
        jnp.dot(normalized_first, qkv_full, preferred_element_type=jnp.float32) + proj_shift
    ).astype(jnp.bfloat16)
    split_heads = projected.reshape(images, SEQ, 3, HEADS, HEAD_DIM)
    queries = split_heads[:, :, 0]
    keys_all = split_heads[:, :, 1]
    values_all = split_heads[:, :, 2]
    raw_scores = (
        jnp.einsum("gqhc,gkhc->ghqk", queries, keys_all, preferred_element_type=jnp.float32)
        * score_scale
    )
    attn_probs = softmax_rows(raw_scores)
    weights = attn_probs.astype(jnp.bfloat16)
    attended = jnp.einsum(
        "ghqk,gkhc->gqhc", weights, values_all, preferred_element_type=jnp.float32
    )
    attended = attended.astype(jnp.bfloat16).reshape(tok_count, feature_count)
    branch = jnp.dot(attended, out_full, preferred_element_type=jnp.float32) + out_shift.astype(
        jnp.float32
    )
    resid_mid = resid_in + branch
    normalized_second, standardized_second, inverse_deviation_second = layer_norm_apply(
        resid_mid, gain_two.astype(jnp.float32), shift_two.astype(jnp.float32)
    )
    normalized_second = normalized_second.astype(jnp.bfloat16)
    logits = jnp.dot(normalized_second, router_full, preferred_element_type=jnp.float32)
    gate_probs = softmax_rows(logits)
    picked = jnp.take_along_axis(gate_probs, routes, 1)
    expert_ids = jnp.arange(experts, dtype=jnp.int32)
    flat_routes = routes.reshape(-1)
    member = (flat_routes[:, None] == expert_ids[None, :]).astype(jnp.int32)
    before = jnp.cumsum(member, 0) - member
    slot_index = jnp.sum(before * member, 1)
    capacity = max(2, (8 * tok_count + 3 * experts - 1) // (3 * experts))
    flat_place = flat_routes * capacity + slot_index
    sent_rows = jnp.broadcast_to(
        normalized_second[:, None, :], (tok_count, 2, feature_count)
    ).reshape(-1, feature_count)
    outbox = (
        jnp.zeros((experts * capacity, feature_count), jnp.bfloat16).at[flat_place].set(sent_rows)
    )
    in_rows = lax.all_to_all(
        outbox.reshape(experts, capacity, feature_count),
        "expert",
        split_axis=0,
        concat_axis=0,
        tiled=True,
    )
    in_rows = lax.all_gather(in_rows.reshape(-1, feature_count), "fsdp", axis=0, tiled=True)
    grad_out = cotangent.astype(jnp.float32)
    grad_slot = (
        (picked[:, :, None] * grad_out[:, None, :]).astype(jnp.bfloat16).reshape(-1, feature_count)
    )
    slot_box = (
        jnp.zeros((experts * capacity, feature_count), jnp.bfloat16).at[flat_place].set(grad_slot)
    )
    grad_inbox = exchange(slot_box.reshape(experts, capacity, feature_count), "expert")
    grad_inbox = lax.all_gather(
        grad_inbox.reshape(-1, feature_count), "fsdp", axis=0, tiled=True
    )
    pair_out = jnp.dot(in_rows, up_full, preferred_element_type=jnp.float32)
    hidden, gated_back = jax.vjp(gated_unit, pair_out)
    hidden = hidden.astype(jnp.bfloat16)
    expert_out = matmul_transposed(hidden, down_full).astype(jnp.bfloat16)
    expert_out = sum_blocks(expert_out.reshape(fsdp, -1, feature_count), "fsdp")
    returned = exchange(
        expert_out.astype(jnp.bfloat16).reshape(experts, capacity, feature_count), "expert"
    ).reshape(-1, feature_count)
    chosen = returned[flat_place].reshape(tok_count, 2, feature_count).astype(jnp.float32)
    mixed_out = resid_mid + jnp.sum(picked[:, :, None] * chosen, 1)
    grad_pick = jnp.sum(grad_out[:, None, :] * chosen, 2)
    grad_hidden = jnp.dot(grad_inbox, down_full, preferred_element_type=jnp.float32)
    down_term = transposed_matmul(grad_inbox, hidden).astype(jnp.bfloat16)
    down_weight_grad = exchange(down_term.reshape(fsdp, shard_rows, shard_width), "fsdp")
    down_weight_grad = (
        down_weight_grad.transpose(1, 0, 2)
        .reshape(1, shard_rows, hidden_width)
        .astype(jnp.float32)
    )
    grad_pairs = gated_back(grad_hidden)[0].astype(jnp.bfloat16)
    grad_rows = matmul_transposed(grad_pairs, up_full).astype(jnp.bfloat16)
    grad_rows = sum_blocks(grad_rows.reshape(fsdp, -1, feature_count), "fsdp")
    grad_returned = exchange(
        grad_rows.astype(jnp.bfloat16).reshape(experts, capacity, feature_count), "expert"
    ).reshape(-1, feature_count)
    up_term = transposed_matmul(in_rows, grad_pairs).astype(jnp.bfloat16)
    gate_up_grad = exchange(up_term.reshape(fsdp, shard_rows, 2 * shard_width), "fsdp")
    gate_up_grad = (
        gate_up_grad.reshape(fsdp, shard_rows, 2, shard_width)
        .transpose(1, 2, 0, 3)
        .reshape(1, shard_rows, 2, hidden_width)
        .astype(jnp.float32)
    )
    grad_expert = jnp.sum(
        grad_returned[flat_place].reshape(tok_count, 2, feature_count).astype(jnp.float32), 1
    )
    route_match = (routes[:, :, None] == expert_ids[None, None, :]).astype(jnp.float32)
    grad_gates = jnp.sum(grad_pick[:, :, None] * route_match, 1)
    grad_logits = gate_probs * (grad_gates - jnp.sum(gate_probs * grad_gates, -1, keepdims=True))
    grad_logits = grad_logits.astype(jnp.bfloat16)
    router_grad = transposed_matmul(grad_logits, normalized_second)
    gradient_normalized_second = matmul_transposed(grad_logits, router_full) + grad_expert
    grad_mid, ln2_gain_grad, ln2_bias_grad = norm_backward(
        gradient_normalized_second,
        gain_two.astype(jnp.float32),
        standardized_second,
        inverse_deviation_second,
    )
    grad_resid = grad_out + grad_mid
    grad_branch = grad_resid.astype(jnp.bfloat16)
    out_weight_grad = transposed_matmul(attended, grad_branch)
    out_bias_grad = jnp.sum(grad_branch.astype(jnp.float32), 0)
    grad_attended = matmul_transposed(grad_branch, out_full).astype(jnp.bfloat16)
    grad_attended = grad_attended.reshape(images, SEQ, HEADS, HEAD_DIM)
    grad_weights = jnp.einsum(
        "gqhc,gkhc->ghqk", grad_attended, values_all, preferred_element_type=jnp.float32
    )
    grad_scores = attn_probs * (
        grad_weights - jnp.sum(attn_probs * grad_weights, -1, keepdims=True)
    )
    grad_scores = grad_scores.astype(jnp.bfloat16)
    grad_value = jnp.einsum(
        "ghqk,gqhc->gkhc", weights, grad_attended, preferred_element_type=jnp.float32
    )
    grad_query = (
        jnp.einsum("ghqk,gkhc->gqhc", grad_scores, keys_all, preferred_element_type=jnp.float32)
        * score_scale
    )
    grad_key = (
        jnp.einsum("ghqk,gqhc->gkhc", grad_scores, queries, preferred_element_type=jnp.float32)
        * score_scale
    )
    grad_proj = jnp.stack([grad_query, grad_key, grad_value], 2).astype(jnp.bfloat16)
    grad_proj = grad_proj.reshape(tok_count, 3 * feature_count)
    qkv_grad = transposed_matmul(normalized_first, grad_proj)
    query_grad = jnp.sum(grad_proj[:, :feature_count].astype(jnp.float32), 0)
    value_grad = jnp.sum(grad_proj[:, 2 * feature_count :].astype(jnp.float32), 0)
    gradient_normalized_first = matmul_transposed(grad_proj, qkv_full)
    grad_first, ln1_gain_grad, ln1_bias_grad = norm_backward(
        gradient_normalized_first,
        gain_one.astype(jnp.float32),
        standardized_first,
        inverse_deviation_first,
    )
    token_grad = grad_resid + grad_first
    vector_grads = jnp.stack(
        [
            ln1_gain_grad,
            ln1_bias_grad,
            query_grad,
            value_grad,
            out_bias_grad,
            ln2_gain_grad,
            ln2_bias_grad,
        ]
    )
    small_part = owners_sum_columns(jnp.concatenate([router_grad, vector_grads]))
    router_part = small_part[:experts].T
    (
        ln1_gain_part,
        ln1_bias_part,
        query_part,
        value_part,
        out_bias_part,
        ln2_gain_part,
        ln2_bias_part,
    ) = small_part[experts:]
    out_weight_part = owners_sum(out_weight_grad)
    qkv_part = owners_sum(qkv_grad)
    return (
        mixed_out.astype(jnp.bfloat16),
        token_grad,
        ln1_gain_part,
        ln1_bias_part,
        qkv_part,
        query_part,
        value_part,
        out_weight_part,
        out_bias_part,
        ln2_gain_part,
        ln2_bias_part,
        router_part,
        gate_up_grad,
        down_weight_grad,
    )


def solution(mesh):
    placed = (
        P(("fsdp", "expert"), None),
        P(("fsdp", "expert"), None),
        P(("fsdp", "expert"), None),
        P(("fsdp", "expert")),
        P(("fsdp", "expert")),
        P(("fsdp", "expert"), None),
        P(("fsdp", "expert")),
        P(("fsdp", "expert")),
        P(("fsdp", "expert"), None),
        P(("fsdp", "expert")),
        P(("fsdp", "expert")),
        P(("fsdp", "expert")),
        P(("fsdp", "expert"), None),
        P("expert", "fsdp", None, None),
        P("expert", "fsdp", None),
    )
    return jax.shard_map(
        per_device,
        mesh=mesh,
        in_specs=placed,
        out_specs=(
            P(("fsdp", "expert"), None),
            P(("fsdp", "expert"), None),
            P(("fsdp", "expert")),
            P(("fsdp", "expert")),
            P(("fsdp", "expert"), None),
            P(("fsdp", "expert")),
            P(("fsdp", "expert")),
            P(("fsdp", "expert"), None),
            P(("fsdp", "expert")),
            P(("fsdp", "expert")),
            P(("fsdp", "expert")),
            P(("fsdp", "expert"), None),
            P("expert", "fsdp", None, None),
            P("expert", "fsdp", None),
        ),
        check_vma=False,
    )
```

```python
import jax
import jax.numpy as jnp
from jax import lax
from jax.sharding import PartitionSpec as P

HEADS = 12
HEAD_DIM = 64
SEQ = 197


EPSILON = 1e-06


def matmul_transposed(first_op, second_op):
    return lax.dot_general(
        first_op, second_op, (((1,), (1,)), ((), ())), preferred_element_type=jnp.float32
    )


def transposed_matmul(first_op, second_op):
    return lax.dot_general(
        first_op, second_op, (((0,), (0,)), ((), ())), preferred_element_type=jnp.float32
    )


def softmax_rows(scores):
    largest = jnp.max(scores, -1, keepdims=True)
    raised = jnp.exp(scores - largest)
    return raised / jnp.sum(raised, -1, keepdims=True)


def layer_norm_apply(values, gain_vec, shift_vec):
    row_mean = jnp.mean(values, -1, keepdims=True)
    centered = values - row_mean
    inv_std = lax.rsqrt(jnp.mean(centered * centered, -1, keepdims=True) + EPSILON)
    normed = centered * inv_std
    return (normed * gain_vec + shift_vec, normed, inv_std)


def norm_backward(grad_in, gain_vec, normed, inv_std):
    scaled = grad_in * gain_vec
    mean_one = jnp.mean(scaled, -1, keepdims=True)
    mean_two = jnp.mean(scaled * normed, -1, keepdims=True)
    grad_values = inv_std * (scaled - mean_one - normed * mean_two)
    return (grad_values, jnp.sum(grad_in * normed, 0), jnp.sum(grad_in, 0))


def gated_unit(pair_out):
    half_width = pair_out.shape[1] // 2
    return jax.nn.gelu(pair_out[:, :half_width], approximate=False) * pair_out[:, half_width:]


def exchange(blocks, axis_name):
    return lax.all_to_all(blocks, axis_name, split_axis=0, concat_axis=0, tiled=True)


def ring_exchange(blocks, axis_name):
    count = blocks.shape[0]
    me = lax.axis_index(axis_name)
    got = [lax.dynamic_index_in_dim(blocks, me, 0, keepdims=False)]
    for shift in range(1, count):
        block = lax.dynamic_index_in_dim(blocks, (me + shift) % count, 0, keepdims=False)
        pairs = [(source, (source + shift) % count) for source in range(count)]
        got.append(lax.ppermute(block, axis_name, pairs))
    return got


def ring_sum_blocks(blocks, axis_name):
    return sum(block.astype(jnp.float32) for block in ring_exchange(blocks, axis_name))


def ring_ordered(got, axis_name):
    count = len(got)
    me = lax.axis_index(axis_name)
    got = jnp.stack(got)
    return [
        lax.dynamic_index_in_dim(got, (me - source + count) % count, 0, keepdims=False)
        for source in range(count)
    ]


def sum_blocks(blocks, axis_name):
    return jnp.sum(exchange(blocks, axis_name).astype(jnp.float32), 0)


def owners_sum(grad):
    outer, inner = lax.axis_size("fsdp"), lax.axis_size("expert")
    rows = grad.shape[0] // (outer * inner)
    parts = grad.astype(jnp.bfloat16).reshape(outer, inner, rows, grad.shape[1])
    half = sum_blocks(parts.transpose(1, 0, 2, 3), "expert")
    return sum_blocks(half.astype(jnp.bfloat16), "fsdp")


def owners_sum_columns(grad):
    outer, inner = lax.axis_size("fsdp"), lax.axis_size("expert")
    count = grad.shape[0]
    parts = grad.reshape(count, outer, inner, grad.shape[1] // (outer * inner))
    half = sum_blocks(parts.transpose(2, 1, 0, 3), "expert")
    return sum_blocks(half, "fsdp")


def per_device(
    tokens,
    cotangent,
    routes,
    ln1_gain,
    ln1_bias,
    qkv_weight,
    query_bias,
    value_bias,
    out_weight,
    out_bias,
    ln2_gain,
    ln2_bias,
    router_weight,
    gate_up,
    down_weight,
):
    tok_count = tokens.shape[0]
    feature_count = tokens.shape[1]
    images = tok_count // SEQ
    score_scale = HEAD_DIM ** (-0.5)
    fsdp = lax.axis_size("fsdp")
    qkv_width, out_width = qkv_weight.shape[1], out_weight.shape[1]
    experts = router_weight.shape[1]
    hidden_width = gate_up.shape[3]
    shard_width = hidden_width // fsdp
    shard_rows = gate_up.shape[1]
    vectors = jnp.stack(
        [ln1_gain, ln1_bias, query_bias, value_bias, out_bias, ln2_gain, ln2_bias], 1
    )
    small = jnp.concatenate([router_weight, vectors], 1)
    small = jnp.pad(small, ((0, 0), (0, -small.shape[1] % 128)))
    packed = lax.all_gather(
        jnp.concatenate([qkv_weight, out_weight, small], 1),
        ("fsdp", "expert"),
        axis=0,
        tiled=True,
    )
    def part_of(rows, index):
        return rows[:, index * shard_width : (index + 1) * shard_width]

    up_parts = jnp.stack(
        [
            jnp.concatenate(
                [part_of(gate_up[0, :, 0], index), part_of(gate_up[0, :, 1], index)], 1
            )
            for index in range(fsdp)
        ]
    )
    up_full = exchange(up_parts, "fsdp").reshape(feature_count, 2 * shard_width)
    down_parts = jnp.stack([part_of(down_weight[0], index) for index in range(fsdp)])
    down_full = exchange(down_parts, "fsdp").reshape(feature_count, shard_width)
    packed, up_full = lax.optimization_barrier((packed, up_full))
    qkv_full = packed[:, :qkv_width]
    out_full = packed[:, qkv_width : qkv_width + out_width]
    small_full = packed[:, qkv_width + out_width :]
    router_full = small_full[:, :experts]
    gain_one, shift_one, query_shift, value_shift, out_shift, gain_two, shift_two = (
        small_full[:, experts : experts + 7].T
    )
    resid_in = tokens.astype(jnp.float32)
    normalized_first, standardized_first, inverse_deviation_first = layer_norm_apply(
        resid_in, gain_one.astype(jnp.float32), shift_one.astype(jnp.float32)
    )
    normalized_first = normalized_first.astype(jnp.bfloat16)
    proj_shift = jnp.concatenate([query_shift, jnp.zeros_like(query_shift), value_shift]).astype(
        jnp.float32
    )
    projected = (
        jnp.dot(normalized_first, qkv_full, preferred_element_type=jnp.float32) + proj_shift
    ).astype(jnp.bfloat16)
    split_heads = projected.reshape(images, SEQ, 3, HEADS, HEAD_DIM)
    queries = split_heads[:, :, 0]
    keys_all = split_heads[:, :, 1]
    values_all = split_heads[:, :, 2]
    raw_scores = (
        jnp.einsum("gqhc,gkhc->ghqk", queries, keys_all, preferred_element_type=jnp.float32)
        * score_scale
    )
    attn_probs = softmax_rows(raw_scores)
    weights = attn_probs.astype(jnp.bfloat16)
    attended = jnp.einsum(
        "ghqk,gkhc->gqhc", weights, values_all, preferred_element_type=jnp.float32
    )
    attended = attended.astype(jnp.bfloat16).reshape(tok_count, feature_count)
    attended, down_full = lax.optimization_barrier((attended, down_full))
    branch = jnp.dot(attended, out_full, preferred_element_type=jnp.float32) + out_shift.astype(
        jnp.float32
    )
    resid_mid = resid_in + branch
    normalized_second, standardized_second, inverse_deviation_second = layer_norm_apply(
        resid_mid, gain_two.astype(jnp.float32), shift_two.astype(jnp.float32)
    )
    normalized_second = normalized_second.astype(jnp.bfloat16)
    logits = jnp.dot(normalized_second, router_full, preferred_element_type=jnp.float32)
    gate_probs = softmax_rows(logits)
    picked = jnp.take_along_axis(gate_probs, routes, 1)
    expert_ids = jnp.arange(experts, dtype=jnp.int32)
    flat_routes = routes.reshape(-1)
    member = (flat_routes[:, None] == expert_ids[None, :]).astype(jnp.int32)
    before = jnp.cumsum(member, 0) - member
    slot_index = jnp.sum(before * member, 1)
    capacity = max(2, (8 * tok_count + 3 * experts - 1) // (3 * experts))
    flat_place = flat_routes * capacity + slot_index
    sent_rows = jnp.broadcast_to(
        normalized_second[:, None, :], (tok_count, 2, feature_count)
    ).reshape(-1, feature_count)
    outbox = (
        jnp.zeros((experts * capacity, feature_count), jnp.bfloat16).at[flat_place].set(sent_rows)
    )
    in_rows = lax.all_to_all(
        outbox.reshape(experts, capacity, feature_count),
        "expert",
        split_axis=0,
        concat_axis=0,
        tiled=True,
    )
    in_rows = lax.all_gather(in_rows.reshape(-1, feature_count), "fsdp", axis=0, tiled=True)
    grad_out = cotangent.astype(jnp.float32)
    grad_slot = (
        (picked[:, :, None] * grad_out[:, None, :]).astype(jnp.bfloat16).reshape(-1, feature_count)
    )
    slot_box = (
        jnp.zeros((experts * capacity, feature_count), jnp.bfloat16).at[flat_place].set(grad_slot)
    )
    grad_inbox = exchange(slot_box.reshape(experts, capacity, feature_count), "expert")
    grad_inbox = lax.all_gather(
        grad_inbox.reshape(-1, feature_count), "fsdp", axis=0, tiled=True
    )
    pair_out = jnp.dot(in_rows, up_full, preferred_element_type=jnp.float32)
    hidden = gated_unit(pair_out).astype(jnp.bfloat16)
    pair_out, hidden = lax.optimization_barrier((pair_out, hidden))
    unused_hidden, gated_back = jax.vjp(gated_unit, pair_out)
    expert_out = matmul_transposed(hidden, down_full).astype(jnp.bfloat16)
    expert_out = ring_sum_blocks(expert_out.reshape(fsdp, -1, feature_count), "fsdp")
    returned = exchange(
        expert_out.astype(jnp.bfloat16).reshape(experts, capacity, feature_count), "expert"
    ).reshape(-1, feature_count)
    chosen = returned[flat_place].reshape(tok_count, 2, feature_count).astype(jnp.float32)
    mixed_out = resid_mid + jnp.sum(picked[:, :, None] * chosen, 1)
    grad_pick = jnp.sum(grad_out[:, None, :] * chosen, 2)
    grad_hidden = jnp.dot(grad_inbox, down_full, preferred_element_type=jnp.float32)
    down_term = transposed_matmul(grad_inbox, hidden).astype(jnp.bfloat16)
    grad_pairs = gated_back(grad_hidden)[0].astype(jnp.bfloat16)
    grad_rows = matmul_transposed(grad_pairs, up_full).astype(jnp.bfloat16)
    grad_rows = ring_sum_blocks(grad_rows.reshape(fsdp, -1, feature_count), "fsdp")
    up_term = transposed_matmul(in_rows, grad_pairs).astype(jnp.bfloat16)
    grad_rows, up_term, down_term = lax.optimization_barrier(
        (grad_rows.astype(jnp.bfloat16), up_term, down_term)
    )
    down_blocks = ring_exchange(down_term.reshape(fsdp, shard_rows, shard_width), "fsdp")
    up_blocks = ring_exchange(up_term.reshape(fsdp, shard_rows, 2 * shard_width), "fsdp")
    grad_returned = exchange(
        grad_rows.reshape(experts, capacity, feature_count), "expert"
    ).reshape(-1, feature_count)
    grad_expert = jnp.sum(
        grad_returned[flat_place].reshape(tok_count, 2, feature_count).astype(jnp.float32), 1
    )
    route_match = (routes[:, :, None] == expert_ids[None, None, :]).astype(jnp.float32)
    grad_gates = jnp.sum(grad_pick[:, :, None] * route_match, 1)
    grad_logits = gate_probs * (grad_gates - jnp.sum(gate_probs * grad_gates, -1, keepdims=True))
    grad_logits = grad_logits.astype(jnp.bfloat16)
    router_grad = transposed_matmul(grad_logits, normalized_second)
    gradient_normalized_second = matmul_transposed(grad_logits, router_full) + grad_expert
    grad_mid, ln2_gain_grad, ln2_bias_grad = norm_backward(
        gradient_normalized_second,
        gain_two.astype(jnp.float32),
        standardized_second,
        inverse_deviation_second,
    )
    grad_resid = grad_out + grad_mid
    grad_branch = grad_resid.astype(jnp.bfloat16)
    out_weight_grad = transposed_matmul(attended, grad_branch)
    out_bias_grad = jnp.sum(grad_branch.astype(jnp.float32), 0)
    grad_attended = matmul_transposed(grad_branch, out_full).astype(jnp.bfloat16)
    grad_attended = grad_attended.reshape(images, SEQ, HEADS, HEAD_DIM)
    grad_weights = jnp.einsum(
        "gqhc,gkhc->ghqk", grad_attended, values_all, preferred_element_type=jnp.float32
    )
    grad_scores = attn_probs * (
        grad_weights - jnp.sum(attn_probs * grad_weights, -1, keepdims=True)
    )
    grad_scores = grad_scores.astype(jnp.bfloat16)
    grad_value = jnp.einsum(
        "ghqk,gqhc->gkhc", weights, grad_attended, preferred_element_type=jnp.float32
    )
    grad_query = (
        jnp.einsum("ghqk,gkhc->gqhc", grad_scores, keys_all, preferred_element_type=jnp.float32)
        * score_scale
    )
    grad_key = (
        jnp.einsum("ghqk,gqhc->gkhc", grad_scores, queries, preferred_element_type=jnp.float32)
        * score_scale
    )
    grad_proj = jnp.stack([grad_query, grad_key, grad_value], 2).astype(jnp.bfloat16)
    grad_proj = grad_proj.reshape(tok_count, 3 * feature_count)
    grad_proj, down_blocks, up_blocks = lax.optimization_barrier(
        (grad_proj, down_blocks, up_blocks)
    )
    qkv_grad = transposed_matmul(normalized_first, grad_proj)
    query_grad = jnp.sum(grad_proj[:, :feature_count].astype(jnp.float32), 0)
    value_grad = jnp.sum(grad_proj[:, 2 * feature_count :].astype(jnp.float32), 0)
    gradient_normalized_first = matmul_transposed(grad_proj, qkv_full)
    grad_first, ln1_gain_grad, ln1_bias_grad = norm_backward(
        gradient_normalized_first,
        gain_one.astype(jnp.float32),
        standardized_first,
        inverse_deviation_first,
    )
    token_grad = grad_resid + grad_first
    down_blocks = ring_ordered(down_blocks, "fsdp")
    up_blocks = ring_ordered(up_blocks, "fsdp")
    down_weight_grad = jnp.concatenate(down_blocks, 1).astype(jnp.float32)[None]
    gate_up_grad = jnp.stack(
        [
            jnp.concatenate([block[:, :shard_width] for block in up_blocks], 1),
            jnp.concatenate([block[:, shard_width:] for block in up_blocks], 1),
        ],
        1,
    ).astype(jnp.float32)[None]
    vector_grads = jnp.stack(
        [
            ln1_gain_grad,
            ln1_bias_grad,
            query_grad,
            value_grad,
            out_bias_grad,
            ln2_gain_grad,
            ln2_bias_grad,
        ]
    )
    small_part = owners_sum_columns(jnp.concatenate([router_grad, vector_grads]))
    router_part = small_part[:experts].T
    (
        ln1_gain_part,
        ln1_bias_part,
        query_part,
        value_part,
        out_bias_part,
        ln2_gain_part,
        ln2_bias_part,
    ) = small_part[experts:]
    out_weight_part = owners_sum(out_weight_grad)
    qkv_part = owners_sum(qkv_grad)
    return (
        mixed_out.astype(jnp.bfloat16),
        token_grad,
        ln1_gain_part,
        ln1_bias_part,
        qkv_part,
        query_part,
        value_part,
        out_weight_part,
        out_bias_part,
        ln2_gain_part,
        ln2_bias_part,
        router_part,
        gate_up_grad,
        down_weight_grad,
    )


def solution(mesh):
    placed = (
        P(("fsdp", "expert"), None),
        P(("fsdp", "expert"), None),
        P(("fsdp", "expert"), None),
        P(("fsdp", "expert")),
        P(("fsdp", "expert")),
        P(("fsdp", "expert"), None),
        P(("fsdp", "expert")),
        P(("fsdp", "expert")),
        P(("fsdp", "expert"), None),
        P(("fsdp", "expert")),
        P(("fsdp", "expert")),
        P(("fsdp", "expert")),
        P(("fsdp", "expert"), None),
        P("expert", "fsdp", None, None),
        P("expert", "fsdp", None),
    )
    return jax.shard_map(
        per_device,
        mesh=mesh,
        in_specs=placed,
        out_specs=(
            P(("fsdp", "expert"), None),
            P(("fsdp", "expert"), None),
            P(("fsdp", "expert")),
            P(("fsdp", "expert")),
            P(("fsdp", "expert"), None),
            P(("fsdp", "expert")),
            P(("fsdp", "expert")),
            P(("fsdp", "expert"), None),
            P(("fsdp", "expert")),
            P(("fsdp", "expert")),
            P(("fsdp", "expert")),
            P(("fsdp", "expert"), None),
            P("expert", "fsdp", None, None),
            P("expert", "fsdp", None),
        ),
        check_vma=False,
    )
```

```python
import jax
import jax.numpy as jnp
from jax import lax
from jax.sharding import PartitionSpec as P

HEADS = 12
HEAD_DIM = 64
SEQ = 197


EPSILON = 1e-06


def matmul_transposed(first_op, second_op):
    return lax.dot_general(
        first_op, second_op, (((1,), (1,)), ((), ())), preferred_element_type=jnp.float32
    )


def transposed_matmul(first_op, second_op):
    return lax.dot_general(
        first_op, second_op, (((0,), (0,)), ((), ())), preferred_element_type=jnp.float32
    )


def softmax_rows(scores):
    largest = jnp.max(scores, -1, keepdims=True)
    raised = jnp.exp(scores - largest)
    return raised / jnp.sum(raised, -1, keepdims=True)


def layer_norm_apply(values, gain_vec, shift_vec):
    row_mean = jnp.mean(values, -1, keepdims=True)
    centered = values - row_mean
    inv_std = lax.rsqrt(jnp.mean(centered * centered, -1, keepdims=True) + EPSILON)
    normed = centered * inv_std
    return (normed * gain_vec + shift_vec, normed, inv_std)


def norm_backward(grad_in, gain_vec, normed, inv_std):
    scaled = grad_in * gain_vec
    mean_one = jnp.mean(scaled, -1, keepdims=True)
    mean_two = jnp.mean(scaled * normed, -1, keepdims=True)
    grad_values = inv_std * (scaled - mean_one - normed * mean_two)
    return (grad_values, jnp.sum(grad_in * normed, 0), jnp.sum(grad_in, 0))


def gated_unit(pair_out):
    half_width = pair_out.shape[1] // 2
    return jax.nn.gelu(pair_out[:, :half_width], approximate=False) * pair_out[:, half_width:]


def exchange(blocks, axis_name):
    return lax.all_to_all(blocks, axis_name, split_axis=0, concat_axis=0, tiled=True)


def ring_exchange(blocks, axis_name):
    count = blocks.shape[0]
    me = lax.axis_index(axis_name)
    got = [lax.dynamic_index_in_dim(blocks, me, 0, keepdims=False)]
    for shift in range(1, count):
        block = lax.dynamic_index_in_dim(blocks, (me + shift) % count, 0, keepdims=False)
        pairs = [(source, (source + shift) % count) for source in range(count)]
        got.append(lax.ppermute(block, axis_name, pairs))
    return got


def ring_sum_blocks(blocks, axis_name):
    return sum(block.astype(jnp.float32) for block in ring_exchange(blocks, axis_name))


def ring_copies(block, axis_name):
    count = lax.axis_size(axis_name)
    got = [block]
    for shift in range(1, count):
        pairs = [(source, (source + shift) % count) for source in range(count)]
        got.append(lax.ppermute(block, axis_name, pairs))
    return got


def place_rows(rows, flat_place, count):
    rows = rows.reshape((-1,) + rows.shape[2:])
    return jnp.zeros((count,) + rows.shape[1:], rows.dtype).at[flat_place].set(rows)


def ring_ordered(got, axis_name):
    count = len(got)
    me = lax.axis_index(axis_name)
    got = jnp.stack(got)
    return [
        lax.dynamic_index_in_dim(got, (me - source + count) % count, 0, keepdims=False)
        for source in range(count)
    ]


def sum_blocks(blocks, axis_name):
    return jnp.sum(exchange(blocks, axis_name).astype(jnp.float32), 0)


def owners_sum(grad):
    outer, inner = lax.axis_size("fsdp"), lax.axis_size("expert")
    rows = grad.shape[0] // (outer * inner)
    parts = grad.astype(jnp.bfloat16).reshape(outer, inner, rows, grad.shape[1])
    half = sum_blocks(parts.transpose(1, 0, 2, 3), "expert")
    return sum_blocks(half.astype(jnp.bfloat16), "fsdp")


def per_device(
    tokens,
    cotangent,
    routes,
    ln1_gain,
    ln1_bias,
    qkv_weight,
    query_bias,
    value_bias,
    out_weight,
    out_bias,
    ln2_gain,
    ln2_bias,
    router_weight,
    gate_up,
    down_weight,
):
    tok_count = tokens.shape[0]
    feature_count = tokens.shape[1]
    images = tok_count // SEQ
    score_scale = HEAD_DIM ** (-0.5)
    fsdp = lax.axis_size("fsdp")
    qkv_width, out_width = qkv_weight.shape[1], out_weight.shape[1]
    experts = router_weight.shape[1]
    hidden_width = gate_up.shape[3]
    shard_width = hidden_width // fsdp
    shard_rows = gate_up.shape[1]
    vectors = jnp.stack(
        [ln1_gain, ln1_bias, query_bias, value_bias, out_bias, ln2_gain, ln2_bias], 1
    )
    small = jnp.concatenate([router_weight, vectors], 1)
    small = jnp.pad(small, ((0, 0), (0, -small.shape[1] % 128)))
    packed = lax.all_gather(
        jnp.concatenate([qkv_weight, out_weight, small], 1),
        ("fsdp", "expert"),
        axis=0,
        tiled=True,
    )
    def part_of(rows, index):
        return rows[:, index * shard_width : (index + 1) * shard_width]

    up_parts = jnp.stack(
        [
            jnp.concatenate(
                [part_of(gate_up[0, :, 0], index), part_of(gate_up[0, :, 1], index)], 1
            )
            for index in range(fsdp)
        ]
    )
    up_full = exchange(up_parts, "fsdp").reshape(feature_count, 2 * shard_width)
    down_parts = jnp.stack([part_of(down_weight[0], index) for index in range(fsdp)])
    down_full = exchange(down_parts, "fsdp").reshape(feature_count, shard_width)
    expert_ids = jnp.arange(experts, dtype=jnp.int32)
    flat_routes = routes.reshape(-1)
    member = (flat_routes[:, None] == expert_ids[None, :]).astype(jnp.int32)
    before = jnp.cumsum(member, 0) - member
    slot_index = jnp.sum(before * member, 1)
    capacity = max(2, (8 * tok_count + 3 * experts - 1) // (3 * experts))
    flat_place = flat_routes * capacity + slot_index
    grad_out = cotangent.astype(jnp.float32)
    cotangent_box = place_rows(
        jnp.broadcast_to(cotangent[:, None, :], (tok_count, 2, feature_count)),
        flat_place,
        experts * capacity,
    )
    cotangent_inbox = exchange(
        cotangent_box.reshape(experts, capacity, feature_count), "expert"
    ).reshape(-1, feature_count)
    cotangent_blocks = ring_copies(cotangent_inbox, "fsdp")
    packed, up_full = lax.optimization_barrier((packed, up_full))
    qkv_full = packed[:, :qkv_width]
    out_full = packed[:, qkv_width : qkv_width + out_width]
    small_full = packed[:, qkv_width + out_width :]
    router_full = small_full[:, :experts]
    gain_one, shift_one, query_shift, value_shift, out_shift, gain_two, shift_two = (
        small_full[:, experts : experts + 7].T
    )
    resid_in = tokens.astype(jnp.float32)
    normalized_first, standardized_first, inverse_deviation_first = layer_norm_apply(
        resid_in, gain_one.astype(jnp.float32), shift_one.astype(jnp.float32)
    )
    normalized_first = normalized_first.astype(jnp.bfloat16)
    proj_shift = jnp.concatenate([query_shift, jnp.zeros_like(query_shift), value_shift]).astype(
        jnp.float32
    )
    projected = (
        jnp.dot(normalized_first, qkv_full, preferred_element_type=jnp.float32) + proj_shift
    ).astype(jnp.bfloat16)
    split_heads = projected.reshape(images, SEQ, 3, HEADS, HEAD_DIM)
    queries = split_heads[:, :, 0]
    keys_all = split_heads[:, :, 1]
    values_all = split_heads[:, :, 2]
    raw_scores = (
        jnp.einsum("gqhc,gkhc->ghqk", queries, keys_all, preferred_element_type=jnp.float32)
        * score_scale
    )
    attn_probs = softmax_rows(raw_scores)
    weights = attn_probs.astype(jnp.bfloat16)
    attended = jnp.einsum(
        "ghqk,gkhc->gqhc", weights, values_all, preferred_element_type=jnp.float32
    )
    attended = attended.astype(jnp.bfloat16).reshape(tok_count, feature_count)
    attended, down_full = lax.optimization_barrier((attended, down_full))
    branch = jnp.dot(attended, out_full, preferred_element_type=jnp.float32) + out_shift.astype(
        jnp.float32
    )
    resid_mid = resid_in + branch
    normalized_second, standardized_second, inverse_deviation_second = layer_norm_apply(
        resid_mid, gain_two.astype(jnp.float32), shift_two.astype(jnp.float32)
    )
    normalized_second = normalized_second.astype(jnp.bfloat16)
    logits = jnp.dot(normalized_second, router_full, preferred_element_type=jnp.float32)
    gate_probs = softmax_rows(logits)
    picked = jnp.take_along_axis(gate_probs, routes, 1)
    sent_rows = jnp.broadcast_to(
        normalized_second[:, None, :], (tok_count, 2, feature_count)
    ).reshape(-1, feature_count)
    outbox = (
        jnp.zeros((experts * capacity, feature_count), jnp.bfloat16).at[flat_place].set(sent_rows)
    )
    in_rows = lax.all_to_all(
        outbox.reshape(experts, capacity, feature_count),
        "expert",
        split_axis=0,
        concat_axis=0,
        tiled=True,
    )
    gates_box = place_rows(picked, flat_place, experts * capacity)
    gates_inbox = exchange(gates_box.reshape(experts, 1, capacity), "expert")
    in_rows, gates_inbox, cotangent_blocks = lax.optimization_barrier(
        (in_rows, gates_inbox, cotangent_blocks)
    )
    in_rows = lax.all_gather(in_rows.reshape(-1, feature_count), "fsdp", axis=0, tiled=True)
    gates_blocks = ring_copies(gates_inbox.reshape(1, -1), "fsdp")
    gates_rows = jnp.concatenate(ring_ordered(gates_blocks, "fsdp"), 1).reshape(-1, 1)
    cotangent_rows = jnp.concatenate(ring_ordered(cotangent_blocks, "fsdp"), 0)
    grad_inbox = (gates_rows * cotangent_rows.astype(jnp.float32)).astype(jnp.bfloat16)
    pair_out = jnp.dot(in_rows, up_full, preferred_element_type=jnp.float32)
    hidden = gated_unit(pair_out).astype(jnp.bfloat16)
    pair_out, hidden = lax.optimization_barrier((pair_out, hidden))
    unused_hidden, gated_back = jax.vjp(gated_unit, pair_out)
    expert_out = matmul_transposed(hidden, down_full).astype(jnp.bfloat16)
    expert_out = ring_sum_blocks(expert_out.reshape(fsdp, -1, feature_count), "fsdp")
    returned = exchange(
        expert_out.astype(jnp.bfloat16).reshape(experts, capacity, feature_count), "expert"
    ).reshape(-1, feature_count)
    chosen = returned[flat_place].reshape(tok_count, 2, feature_count).astype(jnp.float32)
    mixed_out = resid_mid + jnp.sum(picked[:, :, None] * chosen, 1)
    grad_pick = jnp.sum(grad_out[:, None, :] * chosen, 2)
    grad_hidden = jnp.dot(grad_inbox, down_full, preferred_element_type=jnp.float32)
    down_term = transposed_matmul(grad_inbox, hidden).astype(jnp.bfloat16)
    grad_pairs = gated_back(grad_hidden)[0].astype(jnp.bfloat16)
    grad_rows = matmul_transposed(grad_pairs, up_full).astype(jnp.bfloat16)
    grad_rows = ring_sum_blocks(grad_rows.reshape(fsdp, -1, feature_count), "fsdp")
    up_term = transposed_matmul(in_rows, grad_pairs).astype(jnp.bfloat16)
    grad_rows, up_term, down_term = lax.optimization_barrier(
        (grad_rows.astype(jnp.bfloat16), up_term, down_term)
    )
    down_blocks = ring_exchange(down_term.reshape(fsdp, shard_rows, shard_width), "fsdp")
    up_blocks = ring_exchange(up_term.reshape(fsdp, shard_rows, 2 * shard_width), "fsdp")
    grad_returned = exchange(
        grad_rows.reshape(experts, capacity, feature_count), "expert"
    ).reshape(-1, feature_count)
    grad_expert = jnp.sum(
        grad_returned[flat_place].reshape(tok_count, 2, feature_count).astype(jnp.float32), 1
    )
    route_match = (routes[:, :, None] == expert_ids[None, None, :]).astype(jnp.float32)
    grad_gates = jnp.sum(grad_pick[:, :, None] * route_match, 1)
    grad_logits = gate_probs * (grad_gates - jnp.sum(gate_probs * grad_gates, -1, keepdims=True))
    grad_logits = grad_logits.astype(jnp.bfloat16)
    router_grad = transposed_matmul(grad_logits, normalized_second)
    gradient_normalized_second = matmul_transposed(grad_logits, router_full) + grad_expert
    grad_mid, ln2_gain_grad, ln2_bias_grad = norm_backward(
        gradient_normalized_second,
        gain_two.astype(jnp.float32),
        standardized_second,
        inverse_deviation_second,
    )
    grad_resid = grad_out + grad_mid
    grad_branch = grad_resid.astype(jnp.bfloat16)
    out_weight_grad = transposed_matmul(attended, grad_branch)
    out_bias_grad = jnp.sum(grad_branch.astype(jnp.float32), 0)
    grad_attended = matmul_transposed(grad_branch, out_full).astype(jnp.bfloat16)
    grad_attended = grad_attended.reshape(images, SEQ, HEADS, HEAD_DIM)
    grad_weights = jnp.einsum(
        "gqhc,gkhc->ghqk", grad_attended, values_all, preferred_element_type=jnp.float32
    )
    grad_scores = attn_probs * (
        grad_weights - jnp.sum(attn_probs * grad_weights, -1, keepdims=True)
    )
    grad_scores = grad_scores.astype(jnp.bfloat16)
    grad_value = jnp.einsum(
        "ghqk,gqhc->gkhc", weights, grad_attended, preferred_element_type=jnp.float32
    )
    grad_query = (
        jnp.einsum("ghqk,gkhc->gqhc", grad_scores, keys_all, preferred_element_type=jnp.float32)
        * score_scale
    )
    grad_key = (
        jnp.einsum("ghqk,gqhc->gkhc", grad_scores, queries, preferred_element_type=jnp.float32)
        * score_scale
    )
    grad_proj = jnp.stack([grad_query, grad_key, grad_value], 2).astype(jnp.bfloat16)
    grad_proj = grad_proj.reshape(tok_count, 3 * feature_count)
    out_weight_part = owners_sum(out_weight_grad)
    grad_proj, down_blocks, up_blocks, out_weight_part = lax.optimization_barrier(
        (grad_proj, down_blocks, up_blocks, out_weight_part)
    )
    qkv_grad = transposed_matmul(normalized_first, grad_proj)
    query_grad = jnp.sum(grad_proj[:, :feature_count].astype(jnp.float32), 0)
    value_grad = jnp.sum(grad_proj[:, 2 * feature_count :].astype(jnp.float32), 0)
    gradient_normalized_first = matmul_transposed(grad_proj, qkv_full)
    grad_first, ln1_gain_grad, ln1_bias_grad = norm_backward(
        gradient_normalized_first,
        gain_one.astype(jnp.float32),
        standardized_first,
        inverse_deviation_first,
    )
    token_grad = grad_resid + grad_first
    down_blocks = ring_ordered(down_blocks, "fsdp")
    up_blocks = ring_ordered(up_blocks, "fsdp")
    down_weight_grad = jnp.concatenate(down_blocks, 1).astype(jnp.float32)[None]
    gate_up_grad = jnp.stack(
        [
            jnp.concatenate([block[:, :shard_width] for block in up_blocks], 1),
            jnp.concatenate([block[:, shard_width:] for block in up_blocks], 1),
        ],
        1,
    ).astype(jnp.float32)[None]
    vector_grads = jnp.stack(
        [
            ln1_gain_grad,
            ln1_bias_grad,
            query_grad,
            value_grad,
            out_bias_grad,
            ln2_gain_grad,
            ln2_bias_grad,
        ]
    )
    small_grads = jnp.concatenate([router_grad, vector_grads]).T
    small_grads = jnp.pad(small_grads, ((0, 0), (0, -small_grads.shape[1] % 128)))
    late_part = owners_sum(
        jnp.concatenate([qkv_grad.astype(jnp.bfloat16), small_grads.astype(jnp.bfloat16)], 1)
    )
    qkv_part = late_part[:, :qkv_width]
    router_part = late_part[:, qkv_width : qkv_width + experts]
    (
        ln1_gain_part,
        ln1_bias_part,
        query_part,
        value_part,
        out_bias_part,
        ln2_gain_part,
        ln2_bias_part,
    ) = late_part[:, qkv_width + experts : qkv_width + experts + 7].T
    return (
        mixed_out.astype(jnp.bfloat16),
        token_grad,
        ln1_gain_part,
        ln1_bias_part,
        qkv_part,
        query_part,
        value_part,
        out_weight_part,
        out_bias_part,
        ln2_gain_part,
        ln2_bias_part,
        router_part,
        gate_up_grad,
        down_weight_grad,
    )


def solution(mesh):
    placed = (
        P(("fsdp", "expert"), None),
        P(("fsdp", "expert"), None),
        P(("fsdp", "expert"), None),
        P(("fsdp", "expert")),
        P(("fsdp", "expert")),
        P(("fsdp", "expert"), None),
        P(("fsdp", "expert")),
        P(("fsdp", "expert")),
        P(("fsdp", "expert"), None),
        P(("fsdp", "expert")),
        P(("fsdp", "expert")),
        P(("fsdp", "expert")),
        P(("fsdp", "expert"), None),
        P("expert", "fsdp", None, None),
        P("expert", "fsdp", None),
    )
    return jax.shard_map(
        per_device,
        mesh=mesh,
        in_specs=placed,
        out_specs=(
            P(("fsdp", "expert"), None),
            P(("fsdp", "expert"), None),
            P(("fsdp", "expert")),
            P(("fsdp", "expert")),
            P(("fsdp", "expert"), None),
            P(("fsdp", "expert")),
            P(("fsdp", "expert")),
            P(("fsdp", "expert"), None),
            P(("fsdp", "expert")),
            P(("fsdp", "expert")),
            P(("fsdp", "expert")),
            P(("fsdp", "expert"), None),
            P("expert", "fsdp", None, None),
            P("expert", "fsdp", None),
        ),
        check_vma=False,
    )
```
